512 devices in a mesh: outer: 32 (over y, z_lo), inner: 16 (over z_hi, x, core).
Axes of the slice: x: 4, y: 4, z: 16 (z_hi: 2, z_lo: 8; z = z_hi * 8 + z_lo), core: 2. Of those that a mesh axis runs over, the one named last changes fastest.
Arguments:
- image_embed: bfloat16 [131072, 768], P(('outer', 'inner')), may hold values from -1 to 1
- text_embed: bfloat16 [131072, 768], P(('outer', 'inner')), may hold values from -1 to 1
- positive: int32 [512, 256], P(('outer', 'inner')), may hold values from 0 to 255, each once within a row
- row_weight: bfloat16 [131072], P(('outer', 'inner')), may hold values from 0.5 to 18
- logit_scale: float32 [1], replicated, may hold values from 10 to 30
Outputs:
- loss: float32 [1], replicated
- scale_grad: float32 [1], replicated
- image_grad: bfloat16 [131072, 768], P(('outer', 'inner'))
- text_grad: bfloat16 [131072, 768], P(('outer', 'inner'))
The draws below stay inside these ranges and needn't reach their ends.
Inputs may be any that keep to these rules, and one draw needn't show every extreme that they name: `positive`: each row of 256 entries names every text row of its block once.
All inputs are finite; a program needn't handle non-finite values.
Results may differ from the reference program's by a relative error of at most 0.0049.
Values may be sent and summed in bfloat16 or wider, within the bound.
A program may use at most 64 MiB of HBM per device.

```python
import math
import jax
import jax.numpy as jnp
from jax import lax

D = 768
ROWS = 256
STEPS = 4
BLOCKS = 512
PAIRS = 131072
N_INNER = 16


def shared_pattern(key):
    temper = jax.random.uniform(jax.random.fold_in(key, 100), (1,), jnp.float32, 10.0, 30.0)
    return temper


def draw_image_embed(key, part):
    key = jax.random.fold_in(key, 1)
    return jnp.clip(0.07 * jax.random.normal(key, (PAIRS, D), jnp.float32), -1.0, 1.0).astype(jnp.bfloat16)


def draw_text_embed(key, part):
    key = jax.random.fold_in(key, 2)
    return jnp.clip(0.07 * jax.random.normal(key, (PAIRS, D), jnp.float32), -1.0, 1.0).astype(jnp.bfloat16)


def draw_row_weight(key, part):
    key = jax.random.fold_in(key, 3)
    growth = math.log(3.0)
    ranking = jnp.arange(PAIRS, dtype=jnp.float32) / PAIRS
    factor = jnp.exp(jax.random.uniform(key, (PAIRS,), jnp.float32, math.log(0.5), math.log(2.0)))
    return (jnp.exp(growth * ranking) * factor).astype(jnp.bfloat16)


def draw_logit_scale(key, part):
    return shared_pattern(key)


def setup_inputs(seed: int = 0) -> dict:
    seeds = jax.random.split(jax.random.key(seed), 6)
    return {
        "image_embed": draw_image_embed(jax.random.fold_in(seeds[5], 71), 0),
        "text_embed": draw_text_embed(jax.random.fold_in(seeds[5], 71), 0),
        "positive": jax.vmap(lambda own: jax.random.permutation(own, ROWS))(jax.random.split(seeds[2], BLOCKS)).reshape((BLOCKS, ROWS)).astype(jnp.int32),
        "row_weight": draw_row_weight(jax.random.fold_in(seeds[5], 71), 0),
        "logit_scale": draw_logit_scale(jax.random.fold_in(seeds[5], 71), 0),
    }


def neighbour(which, offset):
    return (which // N_INNER * N_INNER + (which % N_INNER + offset) % N_INNER).astype(jnp.int32)


def tile_logits(left, right, temper):
    return temper * jnp.dot(left, right.T, precision=lax.Precision.HIGHEST)


def coefficient(logits, row_lse, col_lse, row_w, col_w, diag_mark, factor):
    result_tile = factor * (row_w[:, None] * (jnp.exp(logits - row_lse[:, None]) - diag_mark)
                            + col_w[None, :] * (jnp.exp(logits - col_lse[None, :]) - diag_mark))
    return lax.optimization_barrier(result_tile.astype(jnp.bfloat16)).astype(jnp.float32)


def reference(image_embed, text_embed, positive, row_weight, logit_scale):
    temper = logit_scale[0]
    images = image_embed.astype(jnp.float32).reshape(BLOCKS, ROWS, D)
    texts = text_embed.astype(jnp.float32).reshape(BLOCKS, ROWS, D)
    weights = row_weight.astype(jnp.float32).reshape(BLOCKS, ROWS)
    block_ids = jnp.arange(BLOCKS, dtype=jnp.int32)
    columns = jnp.arange(ROWS, dtype=jnp.int32)

    def marker_of(which):
        return (columns[None, :] == positive[which][:, None]).astype(jnp.float32)

    def forward(which):
        tile_list = [tile_logits(images[which], texts[neighbour(which, offset)], temper) for offset in range(STEPS + 1)]
        row_part = jax.nn.logsumexp(jnp.concatenate(tile_list, axis=1), axis=1)
        col_part = jnp.stack([jax.nn.logsumexp(logit_tile, axis=0) for logit_tile in tile_list])
        return row_part, col_part

    row_lse, col_parts = lax.map(forward, block_ids)
    col_lse = jax.nn.logsumexp(
        jnp.stack([col_parts[neighbour(block_ids, -offset), offset] for offset in range(STEPS + 1)]), axis=0)
    total_weight = jnp.sum(weights)
    factor = PAIRS / (2.0 * total_weight)

    def image_side(which):
        marker = marker_of(which)
        running = jnp.zeros((ROWS, D), jnp.float32)
        home_tile = None
        for offset in range(STEPS + 1):
            partner = neighbour(which, offset)
            logits = tile_logits(images[which], texts[partner], temper)
            if offset == 0:
                home_tile = logits
                diag_mark = marker
            else:
                diag_mark = 0.0
            coef_tile = coefficient(logits, row_lse[which], col_lse[partner], weights[which], weights[partner], diag_mark, factor)
            running = running + jnp.dot(coef_tile, texts[partner], precision=lax.Precision.HIGHEST)
        positive_logit = jnp.sum(home_tile * marker, axis=1)
        column_logit = jnp.sum(home_tile * marker, axis=0)
        loss_part = jnp.sum(weights[which] * (row_lse[which] - positive_logit)) + jnp.sum(weights[which] * (col_lse[which] - column_logit))
        scale_part = jnp.sum(images[which] * running)
        return running, loss_part, scale_part

    def text_side(which):
        running = jnp.zeros((ROWS, D), jnp.float32)
        for offset in range(STEPS + 1):
            source = neighbour(which, -offset)
            logits = tile_logits(images[source], texts[which], temper)
            diag_mark = marker_of(which) if offset == 0 else 0.0
            coef_tile = coefficient(logits, row_lse[source], col_lse[which], weights[source], weights[which], diag_mark, factor)
            running = running + jnp.dot(coef_tile.T, images[source], precision=lax.Precision.HIGHEST)
        return running

    image_sum, loss_parts, scale_parts = lax.map(image_side, block_ids)
    text_sum = lax.map(text_side, block_ids)
    loss = jnp.reshape(jnp.sum(loss_parts) / (2.0 * total_weight), (1,))
    scale_grad = jnp.reshape(jnp.sum(scale_parts) / PAIRS, (1,))
    image_grad = (temper * image_sum).astype(jnp.bfloat16).reshape(PAIRS, D)
    text_grad = (temper * text_sum).astype(jnp.bfloat16).reshape(PAIRS, D)
    return loss, scale_grad, image_grad, text_grad
```

```python
import functools

import jax
import jax.numpy as jnp
from jax import lax
from jax.experimental import pallas as pl
from jax.experimental.pallas import tpu as pltpu
from jax.sharding import PartitionSpec as P

MESH = pl.DeviceIdType.MESH
CHUNKS = 8
REACH = 4
X_SLOT, RELAY = 10, 11
(K_Z, K_XT, K_XI, K_HT, K_HI, K_HX, K_HR, K_C1, K_C2, K_C3, K_C4) = range(11)
LOW = -1e30
F32 = jnp.float32


def loop(low, high, body):
    def step(k, carry):
        body(k)
        return carry

    lax.fori_loop(low, high, step, 0)


def dot_nt(a, b):
    return lax.dot_general(a, b, (((1,), (1,)), ((), ())), preferred_element_type=F32)


def spread(row):
    return jnp.transpose(jnp.broadcast_to(row, (128, row.shape[1])))


def as_row(col):
    return jnp.transpose(col)[0:1]


def kernel(
    rows, n_z, img_ref, txt_ref, pos_ref, w_ref, scale_ref,
    ig_ref, tg_ref, loss_ref, sg_ref,
    blocks, logits, coefs, stat, diag, wcol, ls, rp, early_out, early_z, early, wp, wy, wz, ay, az,
    local_sem, send, recv, ls_s, ls_r, rp_s, rp_r, ez_s, ez_r, ef_s, ef_r, p_s, p_r, y_s, y_r, z_s, z_r,
):
    part = rows // CHUNKS
    outer, inner = lax.axis_index("outer"), lax.axis_index("inner")
    z_low = n_z // 2
    y, z = outer // z_low, (inner // 8) * z_low + outer % z_low
    p = inner % 8
    even = p % 2 == 0
    mate = p + 1 - 2 * (p % 2)
    half = p // 4
    q = p % 4

    def at(p_, z_, y_=None):
        y_ = y if y_ is None else (y_ + 4) % 4
        z_ = (z_ + n_z) % n_z
        return (y_ * z_low + z_ % z_low, (z_ // z_low) * 8 + (p_ + 8) % 8)

    far = at(p, z + z_low)

    def copy(src, dst, s_sem, r_sem, dev):
        return pltpu.make_async_remote_copy(
            src_ref=src, dst_ref=dst, send_sem=s_sem, recv_sem=r_sem, device_id=dev, device_id_type=MESH
        )

    text_in = pltpu.make_async_copy(txt_ref, blocks.at[0], local_sem.at[0])
    image_in = pltpu.make_async_copy(img_ref, blocks.at[5], local_sem.at[1])
    text_in.start()
    image_in.start()
    barrier = pltpu.get_barrier_semaphore()

    def hello(dev):
        pl.semaphore_signal(barrier, inc=1, device_id=dev, device_id_type=MESH)

    loop(1, 8, lambda d: hello(at(p + d, z)))
    loop(1, 4, lambda d: hello(at(p, z, y + d)))
    loop(1, n_z, lambda d: hello(at(p, z + d)))
    pl.semaphore_wait(barrier, 7 + 3 + n_z - 1)
    text_in.wait()
    image_in.wait()

    def chunk_copy(src, dst, k, dev, kind):
        r = pl.ds(pl.multiple_of(k * part, part), part)
        return copy(blocks.at[src, r], blocks.at[dst, r], send.at[kind, k], recv.at[dst, k], dev)

    def arrived(slot, k):
        chunk_copy(slot, slot, k, far, 0).wait_recv()

    crossing = jnp.where(half == 0, 0, 5)
    loop(0, CHUNKS, lambda k: chunk_copy(crossing, X_SLOT, k, far, K_Z).start())

    def send_own(k):
        pl.when(p >= 2)(lambda: chunk_copy(0, 2, k, at(p - 2, z), K_XT).start())
        pl.when(p <= 5)(lambda: chunk_copy(5, 7, k, at(p + 2, z), K_XI).start())
        pl.when(even)(lambda: chunk_copy(5, 6, k, at(mate, z), K_C1).start())
        pl.when(~even)(lambda: chunk_copy(0, 1, k, at(mate, z), K_C1).start())

    loop(0, CHUNKS, send_own)

    weight = w_ref[...]
    wcol[0] = spread(weight)
    wcol[1] = spread(jnp.log(weight))
    wp[p] = jnp.broadcast_to(jnp.sum(weight, axis=1, keepdims=True), (1, 128))
    loop(1, 8, lambda d: copy(wp.at[p], wp.at[p], p_s.at[d], p_r.at[d], at(p + d, z)).start())

    place = pos_ref[...]
    lanes = lax.broadcasted_iota(jnp.int32, (rows, rows), 1)
    subs = lax.broadcasted_iota(jnp.int32, (rows, rows), 0)
    place_col = spread(place.astype(F32)).astype(jnp.int32)[:, 0:1]
    wc = wcol[0]
    w_sub = jnp.concatenate([wc, wc], axis=1)
    diag[0] = jnp.where(lanes == place_col, w_sub + weight, 0.0)
    diag[1] = jnp.where(subs == place, w_sub + weight, 0.0)
    stat[:, 0] = jnp.full((2, rows, 128), LOW, F32)
    stat[:, 1:3] = jnp.zeros((2, 2, rows, 128), F32)
    rp[q] = jnp.full((4, rows), LOW, F32)
    temper = scale_ref[0]

    def tile(side, k):
        own = jnp.where(side == 0, 5, 0)
        other = jnp.where(side == 0, 0, 5) + k
        t = temper * dot_nt(blocks[own], blocks[other])
        logits[side, k] = t
        old = stat[side, 0]
        new = jnp.maximum(old, jnp.max(t, axis=1, keepdims=True))
        keep = jnp.exp(old - new)
        t0, t1 = t[:, :128], t[:, 128:]
        e0, e1 = jnp.exp(t0 - new), jnp.exp(t1 - new)
        stat[side, 0] = new
        stat[side, 1] = stat[side, 1] * keep + (e0 + e1)
        stat[side, 2] = stat[side, 2] * keep + (e0 * t0 + e1 * t1)

    def lse_of(side):
        total = jnp.broadcast_to(jnp.sum(stat[side, 1], axis=1, keepdims=True), (rows, 128))
        return stat[side, 0] + jnp.log(total)

    def hand_2(k, text, image):
        @pl.when(text)
        def _():
            arrived(2, k)
            pl.when(p >= 2)(lambda: chunk_copy(2, 4, k, at(p - 2, z), K_HT).start())
            chunk_copy(2, jnp.where(even, 1, 3), k, at(mate, z), K_C2).start()

        @pl.when(image)
        def _():
            arrived(7, k)
            pl.when(p <= 5)(lambda: chunk_copy(7, 9, k, at(p + 2, z), K_HI).start())
            chunk_copy(7, jnp.where(even, 8, 6), k, at(mate, z), K_C4).start()

    def hand_4(k, text, image):
        @pl.when(text)
        def _():
            arrived(4, k)
            pl.when(even)(lambda: chunk_copy(4, 3, k, at(mate, z), K_C3).start())

        @pl.when(image)
        def _():
            arrived(9, k)
            pl.when(~even)(lambda: chunk_copy(9, 8, k, at(mate, z), K_C3).start())

    loop(0, CHUNKS, lambda k: hand_2(k, p < 6, p > 1))

    def from_plane(d):
        o = (p + d) % 8
        copy(wp.at[o], wp.at[o], p_s.at[8 - d], p_r.at[8 - d], far).wait_recv()

    loop(1, 8, from_plane)
    wy[y] = jnp.sum(wp[...], axis=0)
    loop(1, 4, lambda d: copy(wy.at[y], wy.at[y], y_s.at[0, d], y_r.at[0, d], at(p, z, y + d)).start())

    loop(0, CHUNKS, lambda k: hand_4(k, p < 4, p > 3))

    def from_y(which, buf, d):
        o = (y + d) % 4
        copy(buf.at[o], buf.at[o], y_s.at[which, 4 - d], y_r.at[which, 4 - d], far).wait_recv()

    loop(1, 4, lambda d: from_y(0, wy, d))
    wz[z] = jnp.sum(wy[...], axis=0)
    loop(1, n_z, lambda d: copy(wz.at[z], wz.at[z], z_s.at[0, d], z_r.at[0, d], at(p, z + d)).start())

    def from_z(which, buf, d):
        o = (z + d) % n_z
        copy(buf.at[o], buf.at[o], z_s.at[which, n_z - d], z_r.at[which, n_z - d], far).wait_recv()

    def wait_block(slot):
        loop(0, CHUNKS, lambda k: arrived(slot, k))

    def early_text(k):
        pl.when(k % 2 == 1)(lambda: wait_block(k))
        tile(0, k)

    def early_image(k):
        pl.when(k % 2 == 1)(lambda: wait_block(k + 5))
        tile(1, k)

    n_text = jnp.minimum(REACH, 7 - p) + 1
    n_image = jnp.minimum(REACH, p) + 1
    loop(0, n_text, early_text)
    loop(0, n_image, early_image)
    dl = jnp.sum(jnp.sum(diag[0] * logits[0, 0], axis=0, keepdims=True), axis=1, keepdims=True)

    side_x = 1 - half
    early_out[0:1] = as_row(lse_of(side_x))
    early_out[1:2] = jnp.log(weight)
    copy(early_out, early_z, ez_s, ez_r, far).start()
    copy(early_out, early_z, ez_s, ez_r, far).wait_recv()
    loop(0, 4, lambda j: copy(early_z, early.at[q], ef_s.at[j], ef_r.at[q], at(4 * (1 - half) + j, z)).start())

    loop(1, n_z, lambda d: from_z(0, wz, d))
    total_weight = jnp.sum(wz[...], axis=0)

    def hand_x(k):
        arrived(X_SLOT, k)
        pl.when(p < 2)(lambda: chunk_copy(X_SLOT, 2, k, at(p - 2, z), K_XT).start())
        pl.when(p > 5)(lambda: chunk_copy(X_SLOT, 7, k, at(p + 2, z), K_XI).start())
        pl.when((p >= 2) & (p < 4))(lambda: chunk_copy(X_SLOT, RELAY, k, at(p + 2, z), K_HX).start())
        pl.when((p >= 4) & (p < 6))(lambda: chunk_copy(X_SLOT, RELAY, k, at(p - 2, z), K_HX).start())

    def hand_relay(k):
        @pl.when((p >= 2) & (p < 6))
        def _():
            arrived(RELAY, k)
            pl.when(p >= 4)(lambda: chunk_copy(RELAY, 4, k, at(p + 2, z), K_HR).start())
            pl.when(p < 4)(lambda: chunk_copy(RELAY, 9, k, at(p - 2, z), K_HR).start())

    def late(k):
        pl.when(k < CHUNKS)(lambda: hand_x(k))

        @pl.when((k >= 1) & (k <= CHUNKS))
        def _():
            hand_relay(k - 1)
            hand_2(k - 1, p >= 6, p <= 1)

        pl.when(k >= 2)(lambda: hand_4(k - 2, p >= 4, p <= 3))

    loop(0, CHUNKS + 2, late)

    def late_tile(side, k, t):
        pl.when(k % 2 == 1)(lambda: wait_block(k + 5 * side))
        tile(side, k)
        v = logits[side, k]
        top = jnp.max(v, axis=0, keepdims=True)
        rp[q, pl.ds(t, 1)] = top + jnp.log(jnp.sum(jnp.exp(v - top), axis=0, keepdims=True))

    loop(n_text, REACH + 1, lambda k: late_tile(0, k, p + k - 8))
    loop(n_image, REACH + 1, lambda k: late_tile(1, k, p - k + 4))

    def same_half(d):
        return 4 * half + (q + d) % 4

    loop(1, 4, lambda d: copy(rp.at[q], rp.at[q], rp_s.at[d], rp_r.at[d], at(same_half(d), z)).start())
    row_lse, col_lse = lse_of(0), lse_of(1)
    log_w = wcol[1]
    alpha, beta = row_lse - log_w, col_lse - log_w
    ls[p, 0:1] = as_row(alpha)
    ls[p, 1:2] = as_row(beta)

    def mean_of(side):
        return jnp.sum(stat[side, 2], axis=1, keepdims=True) / jnp.sum(stat[side, 1], axis=1, keepdims=True)

    ls[p, 2:3, 0:128] = jnp.sum(wc * (row_lse + col_lse), axis=0, keepdims=True) - dl
    ls[p, 2:3, 128:256] = jnp.sum(wc * (mean_of(0) + mean_of(1)), axis=0, keepdims=True) - dl
    loop(1, 8, lambda d: copy(ls.at[p], ls.at[p], ls_s.at[d], ls_r.at[d], at(p + d, z)).start())

    def from_ls(d):
        o = (p + d) % 8
        copy(ls.at[o], ls.at[o], ls_s.at[8 - d], ls_r.at[8 - d], far).wait_recv()

    def from_rp(d):
        o = (q + d) % 4
        copy(rp.at[o], rp.at[o], rp_s.at[4 - d], rp_r.at[4 - d], far).wait_recv()

    loop(1, 8, from_ls)
    ay[y] = jnp.sum(ls[:, 2:3, :], axis=0)
    loop(1, 4, lambda d: copy(ay.at[y], ay.at[y], y_s.at[1, d], y_r.at[1, d], at(p, z, y + d)).start())
    loop(1, 4, from_rp)
    loop(0, 4, lambda j: copy(early_z, early.at[j], ef_s.at[j], ef_r.at[j], far).wait_recv())

    def coef(side, k):
        here = (p + k < 8) if side == 0 else (p >= k)
        t = (p + k) % 8 if side == 0 else (p - k + 4) % 8
        t = jnp.where(here, 0, t)
        o = (p + k) % 8 if side == 0 else (p - k + 8) % 8
        parts = [rp[j, pl.ds(t, 1)] for j in range(4)] + [early[t, 0:1]]
        top = functools.reduce(jnp.maximum, parts)
        merged = top + jnp.log(sum(jnp.exp(v - top) for v in parts)) - early[t, 1:2]
        theirs = jnp.where(here, ls[o, 1 - side:2 - side], merged)
        mine = alpha if side == 0 else beta
        v = logits[side, k]
        both = jnp.exp(v - theirs) + jnp.exp(v - jnp.concatenate([mine, mine], axis=1))
        if k == 0:
            both = both - diag[side]
        coefs[side, :, k * rows:(k + 1) * rows] = both.astype(jnp.bfloat16)

    for k in range(REACH + 1):
        coef(0, k)
        coef(1, k)

    loop(1, 4, lambda d: from_y(1, ay, d))
    az[z] = jnp.sum(ay[...], axis=0)
    loop(1, n_z, lambda d: copy(az.at[z], az.at[z], z_s.at[1, d], z_r.at[1, d], at(p, z + d)).start())

    n_pairs = 1.0 * rows * lax.axis_size("outer") * lax.axis_size("inner")
    gain = jnp.broadcast_to((temper * n_pairs) / (2.0 * total_weight[:, 0:1]), (1, blocks.shape[2]))
    for side, out in ((0, ig_ref), (1, tg_ref)):
        other = blocks[5 * side:5 * side + 5].reshape((REACH + 1) * rows, blocks.shape[2])
        acc = jnp.dot(coefs[side], other, preferred_element_type=F32)
        out[...] = (acc * gain).astype(out.dtype)

    def sent(k):
        def done(kind):
            chunk_copy(0, 0, k, far, kind).wait_send()

        for kind in (K_Z, K_XT, K_XI, K_C1, K_C2, K_C3, K_C4):
            done(kind)
        pl.when(p >= 2)(lambda: done(K_HT))
        pl.when(p <= 5)(lambda: done(K_HI))

        @pl.when((p >= 2) & (p < 6))
        def _():
            done(K_HX)
            done(K_HR)

    loop(0, CHUNKS, sent)
    loop(1, 8, lambda d: copy(wp.at[p], wp.at[p], p_s.at[d], p_r.at[d], far).wait_send())
    loop(1, 8, lambda d: copy(ls.at[p], ls.at[p], ls_s.at[d], ls_r.at[d], far).wait_send())
    loop(1, 4, lambda d: copy(rp.at[q], rp.at[q], rp_s.at[d], rp_r.at[d], far).wait_send())
    loop(0, 4, lambda j: copy(early_z, early.at[q], ef_s.at[j], ef_r.at[j], far).wait_send())
    copy(early_out, early_z, ez_s, ez_r, far).wait_send()
    for which, by, bz in ((0, wy, wz), (1, ay, az)):
        loop(1, 4, lambda d: copy(by.at[y], by.at[y], y_s.at[which, d], y_r.at[which, d], far).wait_send())
        loop(1, n_z, lambda d: copy(bz.at[z], bz.at[z], z_s.at[which, d], z_r.at[which, d], far).wait_send())

    loop(1, n_z, lambda d: from_z(1, az, d))
    sums = jnp.sum(az[...], axis=0)
    loss_ref[0] = jnp.max(sums[:, 0:128] / (2.0 * total_weight))
    sg_ref[0] = jnp.max(sums[:, 128:256] / (2.0 * total_weight * temper))


def per_device(image_embed, text_embed, positive, row_weight, logit_scale):
    rows, width = image_embed.shape
    n_z = 16
    vmem = pl.BlockSpec(memory_space=pltpu.VMEM)
    smem = pl.BlockSpec(memory_space=pltpu.SMEM)
    hbm = pl.BlockSpec(memory_space=pl.ANY)
    dma = pltpu.SemaphoreType.DMA
    loss, scale_grad, image_grad, text_grad = (None,) * 4
    image_grad, text_grad, loss, scale_grad = pl.pallas_call(
        functools.partial(kernel, rows, n_z),
        out_shape=[
            jax.ShapeDtypeStruct((rows, width), jnp.bfloat16),
            jax.ShapeDtypeStruct((rows, width), jnp.bfloat16),
            jax.ShapeDtypeStruct((1,), F32),
            jax.ShapeDtypeStruct((1,), F32),
        ],
        in_specs=[hbm, hbm, vmem, vmem, smem],
        out_specs=[vmem, vmem, smem, smem],
        scratch_shapes=[
            pltpu.VMEM((12, rows, width), jnp.bfloat16),
            pltpu.VMEM((2, REACH + 1, rows, rows), F32),
            pltpu.VMEM((2, rows, (REACH + 1) * rows), jnp.bfloat16),
            pltpu.VMEM((2, 3, rows, 128), F32),
            pltpu.VMEM((2, rows, rows), F32),
            pltpu.VMEM((2, rows, 128), F32),
            pltpu.VMEM((8, 4, rows), F32),
            pltpu.VMEM((4, 4, rows), F32),
            pltpu.VMEM((2, rows), F32),
            pltpu.VMEM((2, rows), F32),
            pltpu.VMEM((4, 2, rows), F32),
            pltpu.VMEM((8, 1, 128), F32),
            pltpu.VMEM((4, 1, 128), F32),
            pltpu.VMEM((n_z, 1, 128), F32),
            pltpu.VMEM((4, 1, 256), F32),
            pltpu.VMEM((n_z, 1, 256), F32),
            dma((2,)),
            dma((11, CHUNKS)),
            dma((12, CHUNKS)),
            dma((8,)), dma((8,)),
            dma((4,)), dma((4,)),
            dma, dma,
            dma((4,)), dma((4,)),
            dma((8,)), dma((8,)),
            dma((2, 4)), dma((2, 4)),
            dma((2, n_z)), dma((2, n_z)),
        ],
        compiler_params=pltpu.CompilerParams(
            collective_id=0, has_side_effects=True, vmem_limit_bytes=48 * 2**20
        ),
        name="contrast",
    )(
        image_embed, text_embed, positive,
        row_weight.astype(F32).reshape(1, rows), logit_scale,
    )
    return loss, scale_grad, image_grad, text_grad


def solution(mesh):
    both = ("outer", "inner")
    in_specs = (P(both, None), P(both, None), P(both, None), P(both), P())
    out_specs = (P(), P(), P(both, None), P(both, None))
    return jax.shard_map(per_device, mesh=mesh, in_specs=in_specs, out_specs=out_specs, check_vma=False)
```

```python
import functools

import jax
import jax.numpy as jnp
from jax import lax
from jax.experimental import pallas as pl
from jax.experimental.pallas import tpu as pltpu
from jax.sharding import PartitionSpec as P

MESH = pl.DeviceIdType.MESH
CHUNKS = 4
LAG = 1
REACH = 4
RELAY = 10
(K_Z, K_XT, K_XI, K_HT, K_HI, K_HR, K_C1, K_C2, K_C3, K_C4) = range(10)
LOW = -1e30
F32 = jnp.float32


def loop(low, high, body):
    def step(k, carry):
        body(k)
        return carry

    lax.fori_loop(low, high, step, 0)


def dot_nt(a, b):
    return lax.dot_general(a, b, (((1,), (1,)), ((), ())), preferred_element_type=F32)


def spread(row):
    return jnp.transpose(jnp.broadcast_to(row, (128, row.shape[1])))


def as_row(col):
    return jnp.transpose(col)[0:1]


def kernel(
    rows, n_z, img_ref, txt_ref, pos_hbm, w_hbm, scale_ref,
    ig_ref, tg_ref, loss_ref, sg_ref,
    blocks, logits, coefs, stat, diag, wcol, ls, rp, early_out, early_z, early, wp, wy, wz, ay, az,
    grads, pos_ref, w_ref, local_sem, send, recv, whole, ls_s, ls_r, rp_s, rp_r, ez_s, ez_r, ef_s, ef_r, p_s, p_r, y_s, y_r, z_s, z_r,
):
    part = rows // CHUNKS
    outer, inner = lax.axis_index("outer"), lax.axis_index("inner")
    z_low = n_z // 2
    y, z = outer // z_low, (inner // 8) * z_low + outer % z_low
    p = inner % 8
    even = p % 2 == 0
    mate = p + 1 - 2 * (p % 2)
    half = p // 4
    q = p % 4

    def at(p_, z_, y_=None):
        y_ = y if y_ is None else (y_ + 4) % 4
        z_ = (z_ + n_z) % n_z
        return (y_ * z_low + z_ % z_low, (z_ // z_low) * 8 + (p_ + 8) % 8)

    far = at(p, z + z_low)
    cross = at(6 - p + 2 * (p % 2), z + z_low)

    def far_first(j):
        return n_z // 2 + (j // 2) * (1 - 2 * (j % 2))

    def copy(src, dst, s_sem, r_sem, dev):
        return pltpu.make_async_remote_copy(
            src_ref=src, dst_ref=dst, send_sem=s_sem, recv_sem=r_sem, device_id=dev, device_id_type=MESH
        )

    barrier = pltpu.get_barrier_semaphore()

    def hello(dev):
        pl.semaphore_signal(barrier, inc=1, device_id=dev, device_id_type=MESH)

    hello(cross)
    loop(1, n_z, lambda j: hello(at(p, z + far_first(j))))
    loop(1, 4, lambda d: hello(at(p, z, y + d)))
    loop(1, 8, lambda d: hello(at(p + d, z)))
    text_in = pltpu.make_async_copy(txt_ref, blocks.at[0], local_sem.at[0])
    image_in = pltpu.make_async_copy(img_ref, blocks.at[5], local_sem.at[1])
    text_in.start()
    image_in.start()
    pos_in = pltpu.make_async_copy(pos_hbm, pos_ref, local_sem.at[2])
    w_in = pltpu.make_async_copy(w_hbm, w_ref, local_sem.at[3])
    pos_in.start()
    w_in.start()
    pl.semaphore_wait(barrier, 7 + 3 + n_z)
    text_in.wait()
    image_in.wait()
    pos_in.wait()
    w_in.wait()

    def chunk_copy(src, dst, k, dev, kind):
        r = pl.ds(pl.multiple_of(k * part, part), part)
        return copy(blocks.at[src, r], blocks.at[dst, r], send.at[kind], recv.at[dst, k], dev)

    def last_copy(src, dst, k, dev, kind):
        r = pl.ds(pl.multiple_of(k * part, part), part)
        return copy(blocks.at[src, r], blocks.at[dst, r], send.at[kind], whole.at[dst], dev)

    def arrived(slot, k):
        chunk_copy(slot, slot, k, far, 0).wait_recv()

    def all_arrived(slot):
        copy(blocks.at[slot], blocks.at[slot], send.at[0], whole.at[slot], far).wait_recv()

    crossing = jnp.where(half == 0, 0, 5)
    landing = jnp.where(p < 2, 2, jnp.where(p > 5, 7, RELAY))
    loop(0, CHUNKS, lambda k: chunk_copy(crossing, landing, k, cross, K_Z).start())

    def send_own(k):
        pl.when(p >= 2)(lambda: chunk_copy(0, 2, k, at(p - 2, z), K_XT).start())
        pl.when(p <= 5)(lambda: chunk_copy(5, 7, k, at(p + 2, z), K_XI).start())
        pl.when(even)(lambda: last_copy(5, 6, k, at(mate, z), K_C1).start())
        pl.when(~even)(lambda: last_copy(0, 1, k, at(mate, z), K_C1).start())

    loop(0, CHUNKS, send_own)

    weight = w_ref[...]
    wcol[0] = spread(weight)
    wcol[1] = spread(jnp.log(weight))
    wp[p] = jnp.broadcast_to(jnp.sum(weight, axis=1, keepdims=True), (1, 128))
    loop(1, 8, lambda d: copy(wp.at[p], wp.at[p], p_s, p_r, at(p + d, z)).start())

    place = pos_ref[...]
    lanes = lax.broadcasted_iota(jnp.int32, (rows, rows), 1)
    subs = lax.broadcasted_iota(jnp.int32, (rows, rows), 0)
    place_col = spread(place.astype(F32)).astype(jnp.int32)[:, 0:1]
    wc = wcol[0]
    w_sub = jnp.concatenate([wc, wc], axis=1)
    diag[0] = jnp.where(lanes == place_col, w_sub + weight, 0.0)
    diag[1] = jnp.where(subs == place, w_sub + weight, 0.0)
    stat[:, 0] = jnp.full((2, rows, 128), LOW, F32)
    stat[:, 1:3] = jnp.zeros((2, 2, rows, 128), F32)
    rp[q] = jnp.full((4, rows), LOW, F32)
    temper = scale_ref[0]

    def tile(side, k):
        own = jnp.where(side == 0, 5, 0)
        other = jnp.where(side == 0, 0, 5) + k
        t = temper * dot_nt(blocks[own], blocks[other])
        logits[side, k] = t
        old = stat[side, 0]
        new = jnp.maximum(old, jnp.max(t, axis=1, keepdims=True))
        keep = jnp.exp(old - new)
        t0, t1 = t[:, :128], t[:, 128:]
        e0, e1 = jnp.exp(t0 - new), jnp.exp(t1 - new)
        stat[side, 0] = new
        stat[side, 1] = stat[side, 1] * keep + (e0 + e1)
        stat[side, 2] = stat[side, 2] * keep + (e0 * t0 + e1 * t1)

    def lse_of(side):
        total = jnp.broadcast_to(jnp.sum(stat[side, 1], axis=1, keepdims=True), (rows, 128))
        return stat[side, 0] + jnp.log(total)

    def hand_2(k, text, image):
        @pl.when(text)
        def _():
            arrived(2, k)
            pl.when(p >= 2)(lambda: chunk_copy(2, 4, k, at(p - 2, z), K_HT).start())
            last_copy(2, jnp.where(even, 1, 3), k, at(mate, z), K_C2).start()

        @pl.when(image)
        def _():
            arrived(7, k)
            pl.when(p <= 5)(lambda: chunk_copy(7, 9, k, at(p + 2, z), K_HI).start())
            last_copy(7, jnp.where(even, 8, 6), k, at(mate, z), K_C4).start()

    def hand_4(k, text, image):
        @pl.when(text)
        def _():
            arrived(4, k)
            pl.when(even)(lambda: last_copy(4, 3, k, at(mate, z), K_C3).start())

        @pl.when(image)
        def _():
            arrived(9, k)
            pl.when(~even)(lambda: last_copy(9, 8, k, at(mate, z), K_C3).start())

    loop(0, CHUNKS, lambda k: hand_2(k, p < 6, p > 1))

    copy(wp.at[0:7], wp.at[0:7], p_s, p_r, far).wait_recv()
    wy[y] = jnp.sum(wp[...], axis=0)
    loop(1, 4, lambda d: copy(wy.at[y], wy.at[y], y_s.at[0], y_r.at[0], at(p, z, y + d)).start())

    loop(0, CHUNKS, lambda k: hand_4(k, p < 4, p > 3))

    def from_y(which, buf):
        copy(buf.at[0:3], buf.at[0:3], y_s.at[which], y_r.at[which], far).wait_recv()

    from_y(0, wy)
    wz[z] = jnp.sum(wy[...], axis=0)

    def to_z(which, buf, d):
        copy(buf.at[z], buf.at[z], z_s.at[which], z_r.at[which], at(p, z + d)).start()

    loop(1, n_z, lambda j: to_z(0, wz, far_first(j)))

    def from_z(which, buf):
        copy(buf.at[1:n_z], buf.at[1:n_z], z_s.at[which], z_r.at[which], far).wait_recv()

    def wait_block(slot):
        all_arrived(slot)

    def early_text(k):
        pl.when(k % 2 == 1)(lambda: wait_block(k))
        tile(0, k)

    def early_image(k):
        pl.when(k % 2 == 1)(lambda: wait_block(k + 5))
        tile(1, k)

    n_text = jnp.minimum(REACH, 7 - p) + 1
    n_image = jnp.minimum(REACH, p) + 1
    loop(0, n_text, early_text)
    loop(0, n_image, early_image)
    dl = jnp.sum(jnp.sum(diag[0] * logits[0, 0], axis=0, keepdims=True), axis=1, keepdims=True)

    side_x = 1 - half
    early_out[0:1] = as_row(lse_of(side_x))
    early_out[1:2] = jnp.log(weight)
    copy(early_out, early_z, ez_s, ez_r, far).start()

    def hand_relay(k):
        @pl.when((p >= 2) & (p < 6))
        def _():
            arrived(RELAY, k)
            pl.when(p >= 4)(lambda: chunk_copy(RELAY, 4, k, at(p + 2, z), K_HR).start())
            pl.when(p < 4)(lambda: chunk_copy(RELAY, 9, k, at(p - 2, z), K_HR).start())

    def late(k):
        @pl.when(k < CHUNKS)
        def _():
            hand_relay(k)
            hand_2(k, p >= 6, p <= 1)

        pl.when(k >= LAG)(lambda: hand_4(k - LAG, p >= 4, p <= 3))

    loop(0, CHUNKS + LAG, late)
    copy(early_out, early_z, ez_s, ez_r, far).wait_recv()
    loop(0, 4, lambda j: copy(early_z, early.at[q], ef_s, ef_r, at(4 * (1 - half) + j, z)).start())

    def late_tile(side, k, t):
        pl.when(k % 2 == 1)(lambda: wait_block(k + 5 * side))
        tile(side, k)
        v = logits[side, k]
        top = jnp.max(v, axis=0, keepdims=True)
        rp[q, pl.ds(t, 1)] = top + jnp.log(jnp.sum(jnp.exp(v - top), axis=0, keepdims=True))

    loop(n_text, REACH + 1, lambda k: late_tile(0, k, p + k - 8))
    loop(n_image, REACH + 1, lambda k: late_tile(1, k, p - k + 4))

    def same_half(d):
        return 4 * half + (q + d) % 4

    loop(1, 4, lambda d: copy(rp.at[q], rp.at[q], rp_s, rp_r, at(same_half(d), z)).start())
    row_lse, col_lse = lse_of(0), lse_of(1)
    log_w = wcol[1]
    alpha, beta = row_lse - log_w, col_lse - log_w
    ls[p, 0:1] = as_row(alpha)
    ls[p, 1:2] = as_row(beta)

    def mean_of(side):
        return jnp.sum(stat[side, 2], axis=1, keepdims=True) / jnp.sum(stat[side, 1], axis=1, keepdims=True)

    ls[p, 2:3, 0:128] = jnp.sum(wc * (row_lse + col_lse), axis=0, keepdims=True) - dl
    ls[p, 2:3, 128:256] = jnp.sum(wc * (mean_of(0) + mean_of(1)), axis=0, keepdims=True) - dl
    loop(1, 8, lambda d: copy(ls.at[p], ls.at[p], ls_s, ls_r, at(p + d, z)).start())

    from_z(0, wz)
    total_weight = jnp.sum(wz[...], axis=0)
    n_pairs = 1.0 * rows * lax.axis_size("outer") * lax.axis_size("inner")
    factor = n_pairs / (2.0 * total_weight)
    log_f = jnp.log(factor)
    log_f2 = jnp.concatenate([log_f, log_f], axis=1)

    copy(ls.at[0:7], ls.at[0:7], ls_s, ls_r, far).wait_recv()
    ay[y] = jnp.sum(ls[:, 2:3, :], axis=0)
    loop(1, 4, lambda d: copy(ay.at[y], ay.at[y], y_s.at[1], y_r.at[1], at(p, z, y + d)).start())
    copy(rp.at[0:3], rp.at[0:3], rp_s, rp_r, far).wait_recv()
    copy(early, early, ef_s, ef_r, far).wait_recv()

    def coef(side, k):
        here = (p + k < 8) if side == 0 else (p >= k)
        t = (p + k) % 8 if side == 0 else (p - k + 4) % 8
        t = jnp.where(here, 0, t)
        o = (p + k) % 8 if side == 0 else (p - k + 8) % 8
        parts = [rp[j, pl.ds(t, 1)] for j in range(4)] + [early[t, 0:1]]
        top = functools.reduce(jnp.maximum, parts)
        merged = top + jnp.log(sum(jnp.exp(v - top) for v in parts)) - early[t, 1:2]
        theirs = jnp.where(here, ls[o, 1 - side:2 - side], merged)
        mine = (alpha if side == 0 else beta) - log_f
        theirs = theirs - log_f2
        v = logits[side, k]
        both = jnp.exp(v - theirs) + jnp.exp(v - jnp.concatenate([mine, mine], axis=1))
        if k == 0:
            both = both - diag[side] * factor[:, 0:1]
        coefs[side, :, k * rows:(k + 1) * rows] = both.astype(jnp.bfloat16)

    coef(0, 0)
    coef(1, 0)
    from_y(1, ay)
    az[z] = jnp.sum(ay[...], axis=0)
    loop(1, n_z, lambda j: to_z(1, az, far_first(j)))
    for k in range(1, REACH + 1):
        coef(0, k)
        coef(1, k)

    for side, out in ((0, ig_ref), (1, tg_ref)):
        other = blocks[5 * side:5 * side + 5].reshape((REACH + 1) * rows, blocks.shape[2])
        acc = jnp.dot(coefs[side], other, preferred_element_type=F32)
        grads[side] = (acc * temper).astype(out.dtype)
        pltpu.make_async_copy(grads.at[side], out, local_sem.at[side]).start()

    def sent(kind):
        copy(blocks.at[0], blocks.at[0], send.at[kind], whole.at[0], far).wait_send()

    for kind in (K_Z, K_C1, K_C2, K_C3, K_C4):
        sent(kind)

    @pl.when(p >= 2)
    def _():
        sent(K_XT)
        sent(K_HT)

    @pl.when(p <= 5)
    def _():
        sent(K_XI)
        sent(K_HI)

    pl.when((p >= 2) & (p < 6))(lambda: sent(K_HR))
    copy(wp.at[0:7], wp.at[0:7], p_s, p_r, far).wait_send()
    copy(ls.at[0:7], ls.at[0:7], ls_s, ls_r, far).wait_send()
    copy(rp.at[0:3], rp.at[0:3], rp_s, rp_r, far).wait_send()
    copy(early, early, ef_s, ef_r, far).wait_send()
    copy(early_out, early_z, ez_s, ez_r, far).wait_send()
    for which, by, bz in ((0, wy, wz), (1, ay, az)):
        copy(by.at[0:3], by.at[0:3], y_s.at[which], y_r.at[which], far).wait_send()
        copy(bz.at[1:n_z], bz.at[1:n_z], z_s.at[which], z_r.at[which], far).wait_send()

    from_z(1, az)
    sums = jnp.sum(az[...], axis=0)
    loss_ref[0] = jnp.max(sums[:, 0:128] / (2.0 * total_weight))
    for side, out in ((0, ig_ref), (1, tg_ref)):
        pltpu.make_async_copy(grads.at[side], out, local_sem.at[side]).wait()
    sg_ref[0] = jnp.max(sums[:, 128:256] / (2.0 * total_weight * temper))


def per_device(image_embed, text_embed, positive, row_weight, logit_scale):
    rows, width = image_embed.shape
    n_z = 16
    smem = pl.BlockSpec(memory_space=pltpu.SMEM)
    hbm = pl.BlockSpec(memory_space=pltpu.HBM)
    dma = pltpu.SemaphoreType.DMA
    image_grad, text_grad, loss, scale_grad = pl.pallas_call(
        functools.partial(kernel, rows, n_z),
        out_shape=[
            jax.ShapeDtypeStruct((rows, width), jnp.bfloat16),
            jax.ShapeDtypeStruct((rows, width), jnp.bfloat16),
            jax.ShapeDtypeStruct((1,), F32),
            jax.ShapeDtypeStruct((1,), F32),
        ],
        in_specs=[hbm, hbm, hbm, hbm, smem],
        out_specs=[hbm, hbm, smem, smem],
        scratch_shapes=[
            pltpu.VMEM((11, rows, width), jnp.bfloat16),
            pltpu.VMEM((2, REACH + 1, rows, rows), F32),
            pltpu.VMEM((2, rows, (REACH + 1) * rows), jnp.bfloat16),
            pltpu.VMEM((2, 3, rows, 128), F32),
            pltpu.VMEM((2, rows, rows), F32),
            pltpu.VMEM((2, rows, 128), F32),
            pltpu.VMEM((8, 4, rows), F32),
            pltpu.VMEM((4, 4, rows), F32),
            pltpu.VMEM((2, rows), F32),
            pltpu.VMEM((2, rows), F32),
            pltpu.VMEM((4, 2, rows), F32),
            pltpu.VMEM((8, 1, 128), F32),
            pltpu.VMEM((4, 1, 128), F32),
            pltpu.VMEM((n_z, 1, 128), F32),
            pltpu.VMEM((4, 1, 256), F32),
            pltpu.VMEM((n_z, 1, 256), F32),
            pltpu.VMEM((2, rows, width), jnp.bfloat16),
            pltpu.VMEM((1, rows), jnp.int32),
            pltpu.VMEM((1, rows), F32),
            dma((4,)),
            dma((10,)),
            dma((11, CHUNKS)),
            dma((9,)),
            dma, dma,
            dma, dma,
            dma, dma,
            dma, dma,
            dma, dma,
            dma((2,)), dma((2,)),
            dma((2,)), dma((2,)),
        ],
        compiler_params=pltpu.CompilerParams(
            collective_id=0, has_side_effects=True, vmem_limit_bytes=62 * 2**20
        ),
        name="contrast",
    )(
        image_embed, text_embed, positive,
        row_weight.astype(F32).reshape(1, rows), logit_scale,
    )
    return loss, scale_grad, image_grad, text_grad


def solution(mesh):
    both = ("outer", "inner")
    in_specs = (P(both, None), P(both, None), P(both, None), P(both), P())
    out_specs = (P(), P(), P(both, None), P(both, None))
    return jax.shard_map(per_device, mesh=mesh, in_specs=in_specs, out_specs=out_specs, check_vma=False)
```

```python
import functools

import jax
import jax.numpy as jnp
from jax import lax
from jax.experimental import pallas as pl
from jax.experimental.pallas import tpu as pltpu
from jax.sharding import PartitionSpec as P

MESH = pl.DeviceIdType.MESH
CHUNKS = 8
DUAL = 2
LAG = 2
REACH = 4
RELAY = 10
HANDED_ON = (2, 4, 7, 9, RELAY)
(K_Z, K_XT, K_XI, K_HT, K_HI, K_HR, K_C1, K_C2, K_C3, K_C4, K_D, K_DR) = range(12)
LOW = -1e30
F32 = jnp.float32


def loop(low, high, body):
    def step(k, carry):
        body(k)
        return carry

    lax.fori_loop(low, high, step, 0)


def dot_nt(a, b):
    return lax.dot_general(a, b, (((1,), (1,)), ((), ())), preferred_element_type=F32)


def spread(row):
    return jnp.transpose(jnp.broadcast_to(row, (128, row.shape[1])))


def as_row(col):
    return jnp.transpose(col)[0:1]


def kernel(
    rows, n_z, img_ref, txt_ref, pos_hbm, w_hbm, scale_ref,
    ig_ref, tg_ref, loss_ref, sg_ref,
    blocks, logits, coefs, stat, diag, wcol, ls, rp, early_out, early_z, early, wy, wz, ay, az,
    grads, pos_ref, w_ref, local_sem, send, recv, whole, ls_s, ls_r, rp_s, rp_r, ez_s, ez_r, ef_s, ef_r, y_s, y_r, z_s, z_r,
):
    part = rows // CHUNKS
    outer, inner = lax.axis_index("outer"), lax.axis_index("inner")
    z_low = n_z // 2
    y, z = outer // z_low, (inner // 8) * z_low + outer % z_low
    p = inner % 8
    even = p % 2 == 0
    mate = p + 1 - 2 * (p % 2)
    half = p // 4
    q = p % 4

    def at(p_, z_, y_=None):
        y_ = y if y_ is None else lax.rem(y_, 4)
        if z_ is not z:
            z_ = lax.rem(z_ + n_z, n_z)
        return (y_ * z_low + lax.rem(z_, z_low), lax.div(z_, z_low) * 8 + lax.rem(p_ + 8, 8))

    far = at(p, z + z_low)
    other_core, left, right = at(mate, z), at(p - 2, z), at(p + 2, z)
    cross = at(6 - p + 2 * (p % 2), z + z_low)

    here = y * 8 + p

    def near(e):
        return at(p + lax.rem(e, 8), z, y + lax.div(e, 8))

    def far_first(j):
        return n_z // 2 + lax.div(j, 2) * (1 - 2 * lax.rem(j, 2))

    def copy(src, dst, s_sem, r_sem, dev):
        return pltpu.make_async_remote_copy(
            src_ref=src, dst_ref=dst, send_sem=s_sem, recv_sem=r_sem, device_id=dev, device_id_type=MESH
        )

    barrier = pltpu.get_barrier_semaphore()

    def hello(dev):
        pl.semaphore_signal(barrier, inc=1, device_id=dev, device_id_type=MESH)

    hello(cross)
    loop(1, n_z, lambda j: hello(at(p, z + far_first(j))))
    loop(1, 32, lambda e: hello(near(e)))
    text_in = pltpu.make_async_copy(txt_ref, blocks.at[0], local_sem.at[0])
    image_in = pltpu.make_async_copy(img_ref, blocks.at[5], local_sem.at[1])
    text_in.start()
    image_in.start()
    pos_in = pltpu.make_async_copy(pos_hbm, pos_ref, local_sem.at[2])
    w_in = pltpu.make_async_copy(w_hbm, w_ref, local_sem.at[3])
    pos_in.start()
    w_in.start()
    pl.semaphore_wait(barrier, 31 + n_z)
    text_in.wait()
    image_in.wait()
    pos_in.wait()
    w_in.wait()

    def chunk_copy(src, dst, k, dev, kind, row=None):
        r = pl.ds(pl.multiple_of(k * part, part), part)
        row = HANDED_ON.index(dst) if row is None else row
        return copy(blocks.at[src, r], blocks.at[dst, r], send.at[kind], recv.at[row, k], dev)

    def last_copy(src, dst, k, dev, kind):
        r = pl.ds(pl.multiple_of(k * part, part), part)
        return copy(blocks.at[src, r], blocks.at[dst, r], send.at[kind], whole.at[dst], dev)

    def arrived(slot, k):
        chunk_copy(slot, slot, k, far, 0).wait_recv()

    def all_arrived(slot):
        copy(blocks.at[slot], blocks.at[slot], send.at[0], whole.at[slot], far).wait_recv()

    crossing = jnp.where(half == 0, 0, 5)
    landing = jnp.where(p < 2, 2, jnp.where(p > 5, 7, RELAY))
    landing_row = jnp.where(p < 2, 0, jnp.where(p > 5, 2, 4))
    loop(0, CHUNKS, lambda k: chunk_copy(crossing, landing, k, cross, K_Z, landing_row).start())

    def send_own(k):
        pl.when(p >= 2)(lambda: chunk_copy(0, 2, k, left, K_XT).start())
        pl.when(p <= 5)(lambda: chunk_copy(5, 7, k, right, K_XI).start())
        pl.when(even)(lambda: last_copy(5, 6, k, other_core, K_C1).start())
        pl.when(~even)(lambda: last_copy(0, 1, k, other_core, K_C1).start())

    loop(0, CHUNKS, send_own)

    weight = w_ref[...].astype(F32).reshape(1, rows)
    wcol[0] = spread(weight)
    wcol[1] = spread(jnp.log(weight))
    wy[here] = jnp.broadcast_to(jnp.sum(weight, axis=1, keepdims=True), (1, 128))
    loop(1, 32, lambda e: copy(wy.at[here], wy.at[here], y_s.at[0], y_r.at[0], near(e)).start())

    place = pos_ref[...]
    lanes = lax.broadcasted_iota(jnp.int32, (rows, rows), 1)
    subs = lax.broadcasted_iota(jnp.int32, (rows, rows), 0)
    place_col = spread(place.astype(F32)).astype(jnp.int32)[:, 0:1]
    wc = wcol[0]
    w_sub = jnp.concatenate([wc, wc], axis=1)
    diag[0] = jnp.where(lanes == place_col, w_sub + weight, 0.0)
    diag[1] = jnp.where(subs == place, w_sub + weight, 0.0)
    stat[:, 0] = jnp.full((2, rows, 128), LOW, F32)
    stat[:, 1:3] = jnp.zeros((2, 2, rows, 128), F32)
    rp[q] = jnp.full((4, rows), LOW, F32)
    temper = scale_ref[0]

    def tile(side, k):
        own = jnp.where(side == 0, 5, 0)
        other = jnp.where(side == 0, 0, 5) + k
        t = temper * dot_nt(blocks[own], blocks[other])
        logits[side, k] = t
        old = stat[side, 0]
        new = jnp.maximum(old, jnp.max(t, axis=1, keepdims=True))
        keep = jnp.exp(old - new)
        t0, t1 = t[:, :128], t[:, 128:]
        e0, e1 = jnp.exp(t0 - new), jnp.exp(t1 - new)
        stat[side, 0] = new
        stat[side, 1] = stat[side, 1] * keep + (e0 + e1)
        stat[side, 2] = stat[side, 2] * keep + (e0 * t0 + e1 * t1)

    def lse_of(side):
        total = jnp.broadcast_to(jnp.sum(stat[side, 1], axis=1, keepdims=True), (rows, 128))
        return stat[side, 0] + jnp.log(total)

    def hand_2(k, text, image):
        @pl.when(text)
        def _():
            arrived(2, k)

            @pl.when(p >= 2)
            def _():
                chunk_copy(2, 4, k, left, K_HT).start()
                pl.when(even & (k >= CHUNKS - DUAL))(lambda: last_copy(2, 3, k, at(p - 1, z), K_D).start())

            last_copy(2, jnp.where(even, 1, 3), k, other_core, K_C2).start()

        @pl.when(image)
        def _():
            arrived(7, k)

            @pl.when(p <= 5)
            def _():
                chunk_copy(7, 9, k, right, K_HI).start()
                pl.when(~even & (k >= CHUNKS - DUAL))(lambda: last_copy(7, 8, k, at(p + 1, z), K_D).start())

            last_copy(7, jnp.where(even, 8, 6), k, other_core, K_C4).start()

    def hand_4(k, text, image):
        @pl.when(text)
        def _():
            arrived(4, k)
            pl.when(even & (k < CHUNKS - DUAL))(lambda: last_copy(4, 3, k, other_core, K_C3).start())

        @pl.when(image)
        def _():
            arrived(9, k)
            pl.when(~even & (k < CHUNKS - DUAL))(lambda: last_copy(9, 8, k, other_core, K_C3).start())

    loop(0, CHUNKS, lambda k: hand_2(k, p < 6, p > 1))

    loop(0, CHUNKS, lambda k: hand_4(k, p < 4, p > 3))

    def from_y(which, buf):
        copy(buf.at[1:32], buf.at[1:32], y_s.at[which], y_r.at[which], far).wait_recv()

    from_y(0, wy)
    wz[z] = jnp.sum(wy[...], axis=0)

    def to_z(which, buf, d):
        copy(buf.at[z], buf.at[z], z_s.at[which], z_r.at[which], at(p, z + d)).start()

    loop(1, n_z, lambda j: to_z(0, wz, far_first(j)))

    def from_z(which, buf):
        copy(buf.at[1:n_z], buf.at[1:n_z], z_s.at[which], z_r.at[which], far).wait_recv()

    def wait_block(slot):
        all_arrived(slot)

    def early_text(k):
        pl.when(k % 2 == 1)(lambda: wait_block(k))
        tile(0, k)

    def early_image(k):
        pl.when(k % 2 == 1)(lambda: wait_block(k + 5))
        tile(1, k)

    n_text = jnp.minimum(REACH, 7 - p) + 1
    n_image = jnp.minimum(REACH, p) + 1
    loop(0, n_text, early_text)
    loop(0, n_image, early_image)
    dl = jnp.sum(jnp.sum(diag[0] * logits[0, 0], axis=0, keepdims=True), axis=1, keepdims=True)

    side_x = 1 - half
    early_out[0:1] = as_row(lse_of(side_x))
    early_out[1:2] = jnp.log(weight)
    copy(early_out, early_z, ez_s, ez_r, far).start()

    def hand_relay(k):
        @pl.when((p >= 2) & (p < 6))
        def _():
            arrived(RELAY, k)

            @pl.when(p >= 4)
            def _():
                chunk_copy(RELAY, 4, k, right, K_HR).start()
                pl.when(even & (k >= CHUNKS - DUAL))(lambda: last_copy(RELAY, 3, k, at(p + 3, z), K_DR).start())

            @pl.when(p < 4)
            def _():
                chunk_copy(RELAY, 9, k, left, K_HR).start()
                pl.when(~even & (k >= CHUNKS - DUAL))(lambda: last_copy(RELAY, 8, k, at(p - 3, z), K_DR).start())

    def late(k):
        @pl.when(k < CHUNKS)
        def _():
            hand_relay(k)
            hand_2(k, p >= 6, p <= 1)

        pl.when(k >= LAG)(lambda: hand_4(k - LAG, p >= 4, p <= 3))

    def late_tile(side, k, t):
        pl.when(k % 2 == 1)(lambda: wait_block(k + 5 * side))
        tile(side, k)
        v = logits[side, k]
        top = jnp.max(v, axis=0, keepdims=True)
        rp[q, pl.ds(t, 1)] = top + jnp.log(jnp.sum(jnp.exp(v - top), axis=0, keepdims=True))

    def late_pair(j):
        k = 2 - j % 2 + 2 * (j // 2)
        pl.when(k >= n_text)(lambda: late_tile(0, k, p + k - 8))
        pl.when(k >= n_image)(lambda: late_tile(1, k, p - k + 4))

    loop(0, CHUNKS, late)
    loop(0, 2, late_pair)
    loop(CHUNKS, CHUNKS + LAG, late)
    loop(2, 4, late_pair)

    def same_half(d):
        return 4 * half + (q + d) % 4

    row_lse, col_lse = lse_of(0), lse_of(1)
    def mean_of(side):
        return jnp.sum(stat[side, 2], axis=1, keepdims=True) / jnp.sum(stat[side, 1], axis=1, keepdims=True)

    ay[here, 0:1, 0:128] = jnp.sum(wc * (row_lse + col_lse), axis=0, keepdims=True) - dl
    ay[here, 0:1, 128:256] = jnp.sum(wc * (mean_of(0) + mean_of(1)), axis=0, keepdims=True) - dl
    loop(1, 32, lambda e: copy(ay.at[here], ay.at[here], y_s.at[1], y_r.at[1], near(e)).start())
    loop(1, 4, lambda d: copy(rp.at[q], rp.at[q], rp_s, rp_r, at(same_half(d), z)).start())
    log_w = wcol[1]
    alpha, beta = row_lse - log_w, col_lse - log_w
    ls[p, 0:1] = as_row(alpha)
    ls[p, 1:2] = as_row(beta)
    loop(1, 8, lambda d: copy(ls.at[p], ls.at[p], ls_s, ls_r, at(p + d, z)).start())


    def coef(side, k):
        here = (p + k < 8) if side == 0 else (p >= k)
        t = (p + k) % 8 if side == 0 else (p - k + 4) % 8
        t = jnp.where(here, 0, t)
        o = (p + k) % 8 if side == 0 else (p - k + 8) % 8
        parts = [rp[j, pl.ds(t, 1)] for j in range(4)] + [early[t, 0:1]]
        top = functools.reduce(jnp.maximum, parts)
        merged = top + jnp.log(sum(jnp.exp(v - top) for v in parts)) - early[t, 1:2]
        theirs = jnp.where(here, ls[o, 1 - side:2 - side], merged)
        mine = (alpha if side == 0 else beta) - log_f
        theirs = theirs - log_f2
        v = logits[side, k]
        both = jnp.exp(v - theirs) + jnp.exp(v - jnp.concatenate([mine, mine], axis=1))
        if k == 0:
            both = both - diag[side] * factor[:, 0:1]
        coefs[side, :, k * rows:(k + 1) * rows] = both.astype(jnp.bfloat16)

    from_y(1, ay)
    az[z] = jnp.sum(ay[...], axis=0)
    loop(1, n_z, lambda j: to_z(1, az, far_first(j)))
    copy(early_out, early_z, ez_s, ez_r, far).wait_recv()
    loop(0, 4, lambda j: copy(early_z, early.at[q], ef_s, ef_r, at(4 * (1 - half) + j, z)).start())
    copy(ls.at[0:7], ls.at[0:7], ls_s, ls_r, far).wait_recv()
    copy(rp.at[0:3], rp.at[0:3], rp_s, rp_r, far).wait_recv()
    from_z(0, wz)
    total_weight = jnp.sum(wz[...], axis=0)
    n_pairs = 1.0 * rows * lax.axis_size("outer") * lax.axis_size("inner")
    factor = n_pairs / (2.0 * total_weight)
    log_f = jnp.log(factor)
    log_f2 = jnp.concatenate([log_f, log_f], axis=1)
    copy(early, early, ef_s, ef_r, far).wait_recv()
    for k in range(REACH + 1):
        coef(0, k)
        coef(1, k)

    for side, out in ((0, ig_ref), (1, tg_ref)):
        other = blocks[5 * side:5 * side + 5].reshape((REACH + 1) * rows, blocks.shape[2])
        acc = jnp.dot(coefs[side], other, preferred_element_type=F32)
        grads[side] = (acc * temper).astype(out.dtype)
        pltpu.make_async_copy(grads.at[side], out, local_sem.at[side]).start()

    def sent(kind):
        copy(blocks.at[0], blocks.at[0], send.at[kind], whole.at[0], far).wait_send()

    def sent_part(kind, chunks):
        r = blocks.at[0, pl.ds(0, chunks * part)]
        copy(r, r, send.at[kind], whole.at[0], far).wait_send()

    for kind in (K_Z, K_C1, K_C2, K_C4):
        sent(kind)
    sent_part(K_C3, CHUNKS - DUAL)
    pl.when((p >= 2) & even)(lambda: sent_part(K_D, DUAL))
    pl.when((p <= 5) & ~even)(lambda: sent_part(K_D, DUAL))
    pl.when((p == 4) | (p == 3))(lambda: sent_part(K_DR, DUAL))

    @pl.when(p >= 2)
    def _():
        sent(K_XT)
        sent(K_HT)

    @pl.when(p <= 5)
    def _():
        sent(K_XI)
        sent(K_HI)

    pl.when((p >= 2) & (p < 6))(lambda: sent(K_HR))
    copy(ls.at[0:7], ls.at[0:7], ls_s, ls_r, far).wait_send()
    copy(rp.at[0:3], rp.at[0:3], rp_s, rp_r, far).wait_send()
    copy(early, early, ef_s, ef_r, far).wait_send()
    copy(early_out, early_z, ez_s, ez_r, far).wait_send()
    for which, by, bz in ((0, wy, wz), (1, ay, az)):
        copy(by.at[1:32], by.at[1:32], y_s.at[which], y_r.at[which], far).wait_send()
        copy(bz.at[1:n_z], bz.at[1:n_z], z_s.at[which], z_r.at[which], far).wait_send()

    from_z(1, az)
    sums = jnp.sum(az[...], axis=0)
    loss_ref[0] = jnp.max(sums[:, 0:128] / (2.0 * total_weight))
    for side, out in ((0, ig_ref), (1, tg_ref)):
        pltpu.make_async_copy(grads.at[side], out, local_sem.at[side]).wait()
    sg_ref[0] = jnp.max(sums[:, 128:256] / (2.0 * total_weight * temper))


def per_device(image_embed, text_embed, positive, row_weight, logit_scale):
    rows, width = image_embed.shape
    n_z = 16
    smem = pl.BlockSpec(memory_space=pltpu.SMEM)
    hbm = pl.BlockSpec(memory_space=pltpu.HBM)
    dma = pltpu.SemaphoreType.DMA
    image_grad, text_grad, loss, scale_grad = pl.pallas_call(
        functools.partial(kernel, rows, n_z),
        out_shape=[
            jax.ShapeDtypeStruct((rows, width), jnp.bfloat16),
            jax.ShapeDtypeStruct((rows, width), jnp.bfloat16),
            jax.ShapeDtypeStruct((1,), F32),
            jax.ShapeDtypeStruct((1,), F32),
        ],
        in_specs=[hbm, hbm, hbm, hbm, smem],
        out_specs=[hbm, hbm, smem, smem],
        scratch_shapes=[
            pltpu.VMEM((11, rows, width), jnp.bfloat16),
            pltpu.VMEM((2, REACH + 1, rows, rows), F32),
            pltpu.VMEM((2, rows, (REACH + 1) * rows), jnp.bfloat16),
            pltpu.VMEM((2, 3, rows, 128), F32),
            pltpu.VMEM((2, rows, rows), F32),
            pltpu.VMEM((2, rows, 128), F32),
            pltpu.VMEM((8, 2, rows), F32),
            pltpu.VMEM((4, 4, rows), F32),
            pltpu.VMEM((2, rows), F32),
            pltpu.VMEM((2, rows), F32),
            pltpu.VMEM((4, 2, rows), F32),
            pltpu.VMEM((32, 1, 128), F32),
            pltpu.VMEM((n_z, 1, 128), F32),
            pltpu.VMEM((32, 1, 256), F32),
            pltpu.VMEM((n_z, 1, 256), F32),
            pltpu.VMEM((2, rows, width), jnp.bfloat16),
            pltpu.VMEM((1, rows), jnp.int32),
            pltpu.VMEM((rows,), jnp.bfloat16),
            dma((4,)),
            dma((12,)),
            dma((len(HANDED_ON), CHUNKS)),
            dma((9,)),
            dma, dma,
            dma, dma,
            dma, dma,
            dma, dma,
            dma((2,)), dma((2,)),
            dma((2,)), dma((2,)),
        ],
        compiler_params=pltpu.CompilerParams(
            collective_id=0, has_side_effects=True, vmem_limit_bytes=62 * 2**20
        ),
        name="contrast",
    )(
        image_embed, text_embed, positive,
        row_weight, logit_scale,
    )
    return loss, scale_grad, image_grad, text_grad


def solution(mesh):
    both = ("outer", "inner")
    in_specs = (P(both, None), P(both, None), P(both, None), P(both), P())
    out_specs = (P(), P(), P(both, None), P(both, None))
    return jax.shard_map(per_device, mesh=mesh, in_specs=in_specs, out_specs=out_specs, check_vma=False)
```

```python
import functools

import jax
import jax.numpy as jnp
from jax import lax
from jax.experimental import pallas as pl
from jax.experimental.pallas import tpu as pltpu
from jax.sharding import PartitionSpec as P

MESH = pl.DeviceIdType.MESH
CHUNKS = 8
DUAL = 2
LAG = 2
REACH = 4
RELAY = 10
HANDED_ON = (2, 4, 7, 9, RELAY)
(K_Z, K_XT, K_XI, K_HT, K_HI, K_HR, K_C1, K_C2, K_C3, K_C4, K_D, K_DR) = range(12)
LOW = -1e30
F32 = jnp.float32


def loop(low, high, body):
    def step(k, carry):
        body(k)
        return carry

    lax.fori_loop(low, high, step, 0)


def dot_nt(a, b):
    return lax.dot_general(a, b, (((1,), (1,)), ((), ())), preferred_element_type=F32)


def spread(row):
    return jnp.transpose(jnp.broadcast_to(row, (128, row.shape[1])))


def as_row(col):
    return jnp.transpose(col)[0:1]


def kernel(
    rows, n_z, img_ref, txt_ref, pos_hbm, w_hbm, scale_ref,
    ig_ref, tg_ref, loss_ref, sg_ref,
    blocks, logits, coefs, stat, diag, wcol, ls, rp, early_out, early_z, early, wy, wz, ay, az,
    grads, pos_ref, w_ref, local_sem, send, recv, whole, ls_s, ls_r, rp_s, rp_r, ez_s, ez_r, ef_s, ef_r, y_s, y_r, z_s, z_r,
):
    part = rows // CHUNKS
    outer, inner = lax.axis_index("outer"), lax.axis_index("inner")
    z_low = n_z // 2
    y, z = outer // z_low, (inner // 8) * z_low + outer % z_low
    p = inner % 8
    even = p % 2 == 0
    mate = p + 1 - 2 * (p % 2)
    half = p // 4
    q = p % 4

    def at(p_, z_, y_=None):
        y_ = y if y_ is None else lax.rem(y_, 4)
        if z_ is not z:
            z_ = lax.rem(z_ + n_z, n_z)
        return (y_ * z_low + lax.rem(z_, z_low), lax.div(z_, z_low) * 8 + lax.rem(p_ + 8, 8))

    far = at(p, z + z_low)
    other_core, left, right = at(mate, z), at(p - 2, z), at(p + 2, z)
    cross = at(6 - p + 2 * (p % 2), z + z_low)

    here = y * 8 + p

    def near(e):
        return at(p + e % 8, z, y + e // 8)

    def far_first(j):
        return n_z // 2 + lax.div(j, 2) * (1 - 2 * lax.rem(j, 2))

    def copy(src, dst, s_sem, r_sem, dev):
        return pltpu.make_async_remote_copy(
            src_ref=src, dst_ref=dst, send_sem=s_sem, recv_sem=r_sem, device_id=dev, device_id_type=MESH
        )

    barrier = pltpu.get_barrier_semaphore()

    def hello(dev):
        pl.semaphore_signal(barrier, inc=1, device_id=dev, device_id_type=MESH)

    hello(cross)
    loop(1, n_z, lambda j: hello(at(p, z + far_first(j))))
    loop(1, 32, lambda e: hello(near(e)))
    text_in = pltpu.make_async_copy(txt_ref, blocks.at[0], local_sem.at[0])
    image_in = pltpu.make_async_copy(img_ref, blocks.at[5], local_sem.at[1])
    text_in.start()
    image_in.start()
    pos_in = pltpu.make_async_copy(pos_hbm, pos_ref, local_sem.at[2])
    w_in = pltpu.make_async_copy(w_hbm, w_ref, local_sem.at[3])
    pos_in.start()
    w_in.start()
    pl.semaphore_wait(barrier, 31 + n_z)
    text_in.wait()
    image_in.wait()
    pos_in.wait()
    w_in.wait()

    def chunk_copy(src, dst, k, dev, kind, row=None):
        r = pl.ds(pl.multiple_of(k * part, part), part)
        row = HANDED_ON.index(dst) if row is None else row
        return copy(blocks.at[src, r], blocks.at[dst, r], send.at[kind], recv.at[row, k], dev)

    def last_copy(src, dst, k, dev, kind):
        r = pl.ds(pl.multiple_of(k * part, part), part)
        return copy(blocks.at[src, r], blocks.at[dst, r], send.at[kind], whole.at[dst], dev)

    def arrived(slot, k):
        chunk_copy(slot, slot, k, far, 0).wait_recv()

    def all_arrived(slot):
        copy(blocks.at[slot], blocks.at[slot], send.at[0], whole.at[slot], far).wait_recv()

    crossing = jnp.where(half == 0, 0, 5)
    landing = jnp.where(p < 2, 2, jnp.where(p > 5, 7, RELAY))
    landing_row = jnp.where(p < 2, 0, jnp.where(p > 5, 2, 4))
    loop(0, CHUNKS, lambda k: chunk_copy(crossing, landing, k, cross, K_Z, landing_row).start())

    def send_own(k):
        pl.when(p >= 2)(lambda: chunk_copy(0, 2, k, left, K_XT).start())
        pl.when(p <= 5)(lambda: chunk_copy(5, 7, k, right, K_XI).start())
        pl.when(even)(lambda: last_copy(5, 6, k, other_core, K_C1).start())
        pl.when(~even)(lambda: last_copy(0, 1, k, other_core, K_C1).start())

    loop(0, CHUNKS, send_own)

    weight = w_ref[...].astype(F32).reshape(1, rows)
    wcol[0] = spread(weight)
    wcol[1] = spread(jnp.log(weight))
    wy[here] = jnp.broadcast_to(jnp.sum(weight, axis=1, keepdims=True), (1, 128))
    loop(1, 32, lambda e: copy(wy.at[here], wy.at[here], y_s.at[0], y_r.at[0], near(e)).start())

    place = pos_ref[...]
    lanes = lax.broadcasted_iota(jnp.int32, (rows, rows), 1)
    subs = lax.broadcasted_iota(jnp.int32, (rows, rows), 0)
    place_col = spread(place.astype(F32)).astype(jnp.int32)[:, 0:1]
    wc = wcol[0]
    w_sub = jnp.concatenate([wc, wc], axis=1)
    diag[0] = jnp.where(lanes == place_col, w_sub + weight, 0.0)
    diag[1] = jnp.where(subs == place, w_sub + weight, 0.0)
    stat[:, 0] = jnp.full((2, rows, 128), LOW, F32)
    stat[:, 1:3] = jnp.zeros((2, 2, rows, 128), F32)
    rp[q] = jnp.full((4, rows), LOW, F32)
    temper = scale_ref[0]

    def tile(side, k):
        own = jnp.where(side == 0, 5, 0)
        other = jnp.where(side == 0, 0, 5) + k
        t = temper * dot_nt(blocks[own], blocks[other])
        logits[side, k] = t
        old = stat[side, 0]
        new = jnp.maximum(old, jnp.max(t, axis=1, keepdims=True))
        keep = jnp.exp(old - new)
        t0, t1 = t[:, :128], t[:, 128:]
        e0, e1 = jnp.exp(t0 - new), jnp.exp(t1 - new)
        stat[side, 0] = new
        stat[side, 1] = stat[side, 1] * keep + (e0 + e1)
        stat[side, 2] = stat[side, 2] * keep + (e0 * t0 + e1 * t1)

    def lse_of(side):
        total = jnp.broadcast_to(jnp.sum(stat[side, 1], axis=1, keepdims=True), (rows, 128))
        return stat[side, 0] + jnp.log(total)

    def hand_2(k, text, image):
        @pl.when(text)
        def _():
            arrived(2, k)

            @pl.when(p >= 2)
            def _():
                chunk_copy(2, 4, k, left, K_HT).start()
                pl.when(even & (k >= CHUNKS - DUAL))(lambda: last_copy(2, 3, k, at(p - 1, z), K_D).start())

            last_copy(2, jnp.where(even, 1, 3), k, other_core, K_C2).start()

        @pl.when(image)
        def _():
            arrived(7, k)

            @pl.when(p <= 5)
            def _():
                chunk_copy(7, 9, k, right, K_HI).start()
                pl.when(~even & (k >= CHUNKS - DUAL))(lambda: last_copy(7, 8, k, at(p + 1, z), K_D).start())

            last_copy(7, jnp.where(even, 8, 6), k, other_core, K_C4).start()

    def hand_4(k, text, image):
        @pl.when(text)
        def _():
            arrived(4, k)
            pl.when(even & (k < CHUNKS - DUAL))(lambda: last_copy(4, 3, k, other_core, K_C3).start())

        @pl.when(image)
        def _():
            arrived(9, k)
            pl.when(~even & (k < CHUNKS - DUAL))(lambda: last_copy(9, 8, k, other_core, K_C3).start())

    loop(0, CHUNKS, lambda k: hand_2(k, p < 6, p > 1))

    loop(0, CHUNKS, lambda k: hand_4(k, p < 4, p > 3))

    def from_y(which, buf):
        copy(buf.at[1:32], buf.at[1:32], y_s.at[which], y_r.at[which], far).wait_recv()

    from_y(0, wy)
    wz[z] = jnp.sum(wy[...], axis=0)

    def to_z(which, buf, d):
        copy(buf.at[z], buf.at[z], z_s.at[which], z_r.at[which], at(p, z + d)).start()

    loop(1, n_z, lambda j: to_z(0, wz, far_first(j)))

    def from_z(which, buf):
        copy(buf.at[1:n_z], buf.at[1:n_z], z_s.at[which], z_r.at[which], far).wait_recv()

    def wait_block(slot):
        all_arrived(slot)

    def early_text(k):
        pl.when(k % 2 == 1)(lambda: wait_block(k))
        tile(0, k)

    def early_image(k):
        pl.when(k % 2 == 1)(lambda: wait_block(k + 5))
        tile(1, k)

    n_text = jnp.minimum(REACH, 7 - p) + 1
    n_image = jnp.minimum(REACH, p) + 1
    loop(0, n_text, early_text)
    loop(0, n_image, early_image)
    dl = jnp.sum(jnp.sum(diag[0] * logits[0, 0], axis=0, keepdims=True), axis=1, keepdims=True)

    side_x = 1 - half
    early_out[0:1] = as_row(lse_of(side_x))
    early_out[1:2] = jnp.log(weight)
    copy(early_out, early_z, ez_s, ez_r, far).start()

    def hand_relay(k):
        @pl.when((p >= 2) & (p < 6))
        def _():
            arrived(RELAY, k)

            @pl.when(p >= 4)
            def _():
                chunk_copy(RELAY, 4, k, right, K_HR).start()
                pl.when(even & (k >= CHUNKS - DUAL))(lambda: last_copy(RELAY, 3, k, at(p + 3, z), K_DR).start())

            @pl.when(p < 4)
            def _():
                chunk_copy(RELAY, 9, k, left, K_HR).start()
                pl.when(~even & (k >= CHUNKS - DUAL))(lambda: last_copy(RELAY, 8, k, at(p - 3, z), K_DR).start())

    def late(k):
        @pl.when(k < CHUNKS)
        def _():
            hand_relay(k)
            hand_2(k, p >= 6, p <= 1)

        pl.when(k >= LAG)(lambda: hand_4(k - LAG, p >= 4, p <= 3))

    def late_tile(side, k, t):
        pl.when(k % 2 == 1)(lambda: wait_block(k + 5 * side))
        tile(side, k)
        v = logits[side, k]
        top = jnp.max(v, axis=0, keepdims=True)
        rp[q, pl.ds(t, 1)] = top + jnp.log(jnp.sum(jnp.exp(v - top), axis=0, keepdims=True))

    def late_pair(j):
        k = 2 - j % 2 + 2 * (j // 2)
        pl.when(k >= n_text)(lambda: late_tile(0, k, p + k - 8))
        pl.when(k >= n_image)(lambda: late_tile(1, k, p - k + 4))

    loop(0, CHUNKS, late)
    loop(0, 2, late_pair)
    loop(CHUNKS, CHUNKS + LAG, late)
    loop(2, 4, late_pair)

    def same_half(d):
        return 4 * half + (q + d) % 4

    row_lse, col_lse = lse_of(0), lse_of(1)
    def mean_of(side):
        return jnp.sum(stat[side, 2], axis=1, keepdims=True) / jnp.sum(stat[side, 1], axis=1, keepdims=True)

    ay[here, 0:1, 0:128] = jnp.sum(wc * (row_lse + col_lse), axis=0, keepdims=True) - dl
    ay[here, 0:1, 128:256] = jnp.sum(wc * (mean_of(0) + mean_of(1)), axis=0, keepdims=True) - dl
    for e in range(1, 32):
        copy(ay.at[here], ay.at[here], y_s.at[1], y_r.at[1], near(e)).start()
    loop(1, 4, lambda d: copy(rp.at[q], rp.at[q], rp_s, rp_r, at(same_half(d), z)).start())
    log_w = wcol[1]
    alpha, beta = row_lse - log_w, col_lse - log_w
    ls[p, 0:1] = as_row(alpha)
    ls[p, 1:2] = as_row(beta)
    loop(1, 8, lambda d: copy(ls.at[p], ls.at[p], ls_s, ls_r, at(p + d, z)).start())


    def coef(side, k):
        here = (p + k < 8) if side == 0 else (p >= k)
        t = (p + k) % 8 if side == 0 else (p - k + 4) % 8
        t = jnp.where(here, 0, t)
        o = (p + k) % 8 if side == 0 else (p - k + 8) % 8
        parts = [rp[j, pl.ds(t, 1)] for j in range(4)] + [early[t, 0:1]]
        top = functools.reduce(jnp.maximum, parts)
        merged = top + jnp.log(sum(jnp.exp(v - top) for v in parts)) - early[t, 1:2]
        theirs = jnp.where(here, ls[o, 1 - side:2 - side], merged)
        mine = (alpha if side == 0 else beta) - log_f
        theirs = theirs - log_f2
        v = logits[side, k]
        both = jnp.exp(v - theirs) + jnp.exp(v - jnp.concatenate([mine, mine], axis=1))
        if k == 0:
            both = both - diag[side] * factor[:, 0:1]
        coefs[side, :, k * rows:(k + 1) * rows] = both.astype(jnp.bfloat16)

    from_y(1, ay)
    az[z] = jnp.sum(ay[...], axis=0)
    for j in range(1, n_z):
        to_z(1, az, n_z // 2 + j // 2 * (1 - 2 * (j % 2)))
    copy(early_out, early_z, ez_s, ez_r, far).wait_recv()
    loop(0, 4, lambda j: copy(early_z, early.at[q], ef_s, ef_r, at(4 * (1 - half) + j, z)).start())
    copy(ls.at[0:7], ls.at[0:7], ls_s, ls_r, far).wait_recv()
    copy(rp.at[0:3], rp.at[0:3], rp_s, rp_r, far).wait_recv()
    from_z(0, wz)
    total_weight = jnp.sum(wz[...], axis=0)
    n_pairs = 1.0 * rows * lax.axis_size("outer") * lax.axis_size("inner")
    factor = n_pairs / (2.0 * total_weight)
    log_f = jnp.log(factor)
    log_f2 = jnp.concatenate([log_f, log_f], axis=1)
    copy(early, early, ef_s, ef_r, far).wait_recv()
    for k in range(REACH + 1):
        coef(0, k)
        coef(1, k)

    for side, out in ((0, ig_ref), (1, tg_ref)):
        other = blocks[5 * side:5 * side + 5].reshape((REACH + 1) * rows, blocks.shape[2])
        acc = jnp.dot(coefs[side], other, preferred_element_type=F32)
        grads[side] = (acc * temper).astype(out.dtype)
        pltpu.make_async_copy(grads.at[side], out, local_sem.at[side]).start()

    def sent(kind):
        copy(blocks.at[0], blocks.at[0], send.at[kind], whole.at[0], far).wait_send()

    def sent_part(kind, chunks):
        r = blocks.at[0, pl.ds(0, chunks * part)]
        copy(r, r, send.at[kind], whole.at[0], far).wait_send()

    for kind in (K_Z, K_C1, K_C2, K_C4):
        sent(kind)
    sent_part(K_C3, CHUNKS - DUAL)
    pl.when((p >= 2) & even)(lambda: sent_part(K_D, DUAL))
    pl.when((p <= 5) & ~even)(lambda: sent_part(K_D, DUAL))
    pl.when((p == 4) | (p == 3))(lambda: sent_part(K_DR, DUAL))

    @pl.when(p >= 2)
    def _():
        sent(K_XT)
        sent(K_HT)

    @pl.when(p <= 5)
    def _():
        sent(K_XI)
        sent(K_HI)

    pl.when((p >= 2) & (p < 6))(lambda: sent(K_HR))
    copy(ls.at[0:7], ls.at[0:7], ls_s, ls_r, far).wait_send()
    copy(rp.at[0:3], rp.at[0:3], rp_s, rp_r, far).wait_send()
    copy(early, early, ef_s, ef_r, far).wait_send()
    copy(early_out, early_z, ez_s, ez_r, far).wait_send()
    for which, by, bz in ((0, wy, wz), (1, ay, az)):
        copy(by.at[1:32], by.at[1:32], y_s.at[which], y_r.at[which], far).wait_send()
        copy(bz.at[1:n_z], bz.at[1:n_z], z_s.at[which], z_r.at[which], far).wait_send()

    from_z(1, az)
    sums = jnp.sum(az[...], axis=0)
    loss_ref[0] = jnp.max(sums[:, 0:128] / (2.0 * total_weight))
    for side, out in ((0, ig_ref), (1, tg_ref)):
        pltpu.make_async_copy(grads.at[side], out, local_sem.at[side]).wait()
    sg_ref[0] = jnp.max(sums[:, 128:256] / (2.0 * total_weight * temper))


def per_device(image_embed, text_embed, positive, row_weight, logit_scale):
    rows, width = image_embed.shape
    n_z = 16
    smem = pl.BlockSpec(memory_space=pltpu.SMEM)
    hbm = pl.BlockSpec(memory_space=pltpu.HBM)
    dma = pltpu.SemaphoreType.DMA
    image_grad, text_grad, loss, scale_grad = pl.pallas_call(
        functools.partial(kernel, rows, n_z),
        out_shape=[
            jax.ShapeDtypeStruct((rows, width), jnp.bfloat16),
            jax.ShapeDtypeStruct((rows, width), jnp.bfloat16),
            jax.ShapeDtypeStruct((1,), F32),
            jax.ShapeDtypeStruct((1,), F32),
        ],
        in_specs=[hbm, hbm, hbm, hbm, smem],
        out_specs=[hbm, hbm, smem, smem],
        scratch_shapes=[
            pltpu.VMEM((11, rows, width), jnp.bfloat16),
            pltpu.VMEM((2, REACH + 1, rows, rows), F32),
            pltpu.VMEM((2, rows, (REACH + 1) * rows), jnp.bfloat16),
            pltpu.VMEM((2, 3, rows, 128), F32),
            pltpu.VMEM((2, rows, rows), F32),
            pltpu.VMEM((2, rows, 128), F32),
            pltpu.VMEM((8, 2, rows), F32),
            pltpu.VMEM((4, 4, rows), F32),
            pltpu.VMEM((2, rows), F32),
            pltpu.VMEM((2, rows), F32),
            pltpu.VMEM((4, 2, rows), F32),
            pltpu.VMEM((32, 1, 128), F32),
            pltpu.VMEM((n_z, 1, 128), F32),
            pltpu.VMEM((32, 1, 256), F32),
            pltpu.VMEM((n_z, 1, 256), F32),
            pltpu.VMEM((2, rows, width), jnp.bfloat16),
            pltpu.VMEM((1, rows), jnp.int32),
            pltpu.VMEM((rows,), jnp.bfloat16),
            dma((4,)),
            dma((12,)),
            dma((len(HANDED_ON), CHUNKS)),
            dma((9,)),
            dma, dma,
            dma, dma,
            dma, dma,
            dma, dma,
            dma((2,)), dma((2,)),
            dma((2,)), dma((2,)),
        ],
        compiler_params=pltpu.CompilerParams(
            collective_id=0, has_side_effects=True, vmem_limit_bytes=62 * 2**20
        ),
        name="contrast",
    )(
        image_embed, text_embed, positive,
        row_weight, logit_scale,
    )
    return loss, scale_grad, image_grad, text_grad


def solution(mesh):
    both = ("outer", "inner")
    in_specs = (P(both, None), P(both, None), P(both, None), P(both), P())
    out_specs = (P(), P(), P(both, None), P(both, None))
    return jax.shard_map(per_device, mesh=mesh, in_specs=in_specs, out_specs=out_specs, check_vma=False)
```
